512 devices in a mesh: sect: 8 (over z_hi, core), dom: 64 (over y, x, z_lo).
Axes of the slice: x: 4, y: 4, z: 16 (z_hi: 4, z_lo: 4; z = z_hi * 4 + z_lo), core: 2. Of those that a mesh axis runs over, the one named last changes fastest.
Arguments:
- nodes: bfloat16 [524288, 512], P(('sect', 'dom')), may hold values from -6 to 6
- fine_tiles: bfloat16 [12288, 128, 128], P(('sect', 'dom')), may hold values from -0.3125 to 0.3125
- fine_target: int32 [12288], P(('sect', 'dom')), may hold values from 0 to 7
- fine_source: int32 [12288], P(('sect', 'dom')), may hold values from 0 to 11
- halo_ids: int32 [512, 2, 2], P(('sect', 'dom')), may hold values from 0 to 7
- pool_map: int32 [4096], P(('sect', 'dom')), may hold values from 0 to 5, as said below
- pool_weight: bfloat16 [524288], P(('sect', 'dom')), may hold values from 0.099609375 to 1
- coarse_tiles: bfloat16 [3072, 128, 128], P(('sect', 'dom')), may hold values from -0.3125 to 0.3125
- coarse_target: int32 [3072], P(('sect', 'dom')), may hold values from 0 to 1
- coarse_source: int32 [3072], P(('sect', 'dom')), may hold values from 0 to 5
- weights: bfloat16 [7, 512, 512], P(None, 'dom'), may hold values from -0.25 to 0.25
Outputs:
- fine_out: bfloat16 [524288, 512], P(('sect', 'dom'))
The draws below stay inside these ranges and needn't reach their ends.
Inputs may be any that keep to these rules, and one draw needn't show every extreme that they name: `pool_map`: at most 2 fine blocks of a partition pool into the previous partition and at most 2 into the next; none pool across the ends of a section's chain.
All inputs are finite; a program needn't handle non-finite values.
Results may differ from the reference program's by a relative error of at most 0.019.
Values may be sent and summed in bfloat16 or wider, within the bound.
No kernel may reach another device: no remote copies, remote signals or barrier semaphores. Data moves between devices by JAX's collectives and lax.ppermute only.
A program may use at most 64 MiB of HBM per device.

```python
import math
import jax
import jax.numpy as jnp
from jax import lax

H = 512
BLK = 128
NB = 8
HB = 2
PB = 2
ROUNDS = 2
ET = 24
NC = 2
CT = 6
FINE_NODES = 524288
N_SECT = 8
N_DOM = 64
DEVICES = 512


def draw_pool_map(key, part):
    key = jax.random.fold_in(key, 7)
    order_key, slot_key = jax.random.split(key)
    ranks = jax.vmap(lambda k: jax.random.permutation(k, NB))(jax.random.split(order_key, DEVICES))
    place = jnp.arange(DEVICES, dtype=jnp.int32) % N_DOM
    sides = jnp.where(ranks < PB, 0, jnp.where(ranks < 2 * PB, 2, 1))
    sides = jnp.where((sides == 0) & (place == 0)[:, None], 1, sides)
    sides = jnp.where((sides == 2) & (place == N_DOM - 1)[:, None], 1, sides)
    slots = jax.random.randint(slot_key, (DEVICES, NB), 0, NC)
    return (sides * NC + slots).reshape(-1).astype(jnp.int32)


def plant(values, own_key, low, high):
    extent = values.shape
    spot = [jax.random.randint(jax.random.fold_in(own_key, axis), (), 0, extent[axis]) for axis in range(len(extent))]
    values = values.at[tuple(spot)].set(low)
    longest = extent.index(max(extent))
    spot[longest] = (spot[longest] + 1) % extent[longest]
    return values.at[tuple(spot)].set(high)


def block_scale(stream_key, shape, cuts, least, high):
    gain = 1.0
    for dim, blocks in cuts:
        steps = jax.random.uniform(jax.random.fold_in(jax.random.fold_in(stream_key, 6), dim), (blocks,), jnp.float32, least / len(cuts), high / len(cuts))
        gain = gain * jnp.repeat(jnp.exp(steps), shape[dim] // blocks).reshape((-1,) + (1,) * (len(shape) - 1 - dim))
    return gain


def normal_values(rng, extent, scale, bound, pieces=(), held_as=jnp.bfloat16):
    factor_of = block_scale(rng, extent, pieces, -0.22, 0.18) if pieces else 1.0
    values = jax.random.normal(rng, extent, jnp.float32) * scale * factor_of
    return jnp.minimum(jnp.maximum(values, -bound), bound).astype(held_as)


def setup_inputs(seed: int = 0) -> dict:
    key_list = jax.random.split(jax.random.key(seed), 12)
    nodes = normal_values(key_list[0], (FINE_NODES, H), 1.0, 6.0, ((0, 512),))
    fine_tiles = normal_values(key_list[1], (DEVICES * ET, BLK, BLK), (3 * BLK) ** -0.5, 0.3125, ((0, 512),))
    fine_target = plant(jax.random.randint(key_list[2], (DEVICES * ET,), 0, NB), jax.random.fold_in(key_list[2], 1), 0, NB - 1).astype(jnp.int32)
    fine_source = plant(jax.random.randint(key_list[3], (DEVICES * ET,), 0, NB + 2 * HB), jax.random.fold_in(key_list[3], 1), 0, (NB + 2 * HB) - 1).astype(jnp.int32)
    halo_ids = plant(jax.random.randint(key_list[4], (DEVICES, 2, HB), 0, NB), jax.random.fold_in(key_list[4], 1), 0, NB - 1).astype(jnp.int32)
    pool_map = draw_pool_map(jax.random.fold_in(key_list[11], 71), 0)
    pool_weight = jnp.clip(jnp.exp(math.log(1.0) - 2.306499 * jax.random.uniform(key_list[6], (FINE_NODES,), jnp.float32) ** block_scale(key_list[6], (FINE_NODES,), ((0, 512),), -0.2, 0.2)), 0.099609375, 1.0).astype(jnp.bfloat16)
    coarse_tiles = normal_values(key_list[7], (DEVICES * CT, BLK, BLK), (3 * BLK) ** -0.5, 0.3125, ((0, 512),))
    coarse_target = plant(jax.random.randint(key_list[8], (DEVICES * CT,), 0, NC), jax.random.fold_in(key_list[8], 1), 0, NC - 1).astype(jnp.int32)
    coarse_source = plant(jax.random.randint(key_list[9], (DEVICES * CT,), 0, 3 * NC), jax.random.fold_in(key_list[9], 1), 0, (3 * NC) - 1).astype(jnp.int32)
    weights = normal_values(key_list[10], (7, H, H), H ** -0.5, 0.25, ((1, 64),))
    return dict(nodes=nodes, fine_tiles=fine_tiles, fine_target=fine_target, fine_source=fine_source, halo_ids=halo_ids, pool_map=pool_map, pool_weight=pool_weight, coarse_tiles=coarse_tiles, coarse_target=coarse_target, coarse_source=coarse_source, weights=weights)


def from_prev(arr, sections):
    shaped = arr.reshape((sections, -1) + arr.shape[1:])
    zero = jnp.zeros_like(shaped[:, :1])
    return jnp.concatenate([zero, shaped[:, :-1]], axis=1).reshape(arr.shape)


def from_next(arr, sections):
    shaped = arr.reshape((sections, -1) + arr.shape[1:])
    zero = jnp.zeros_like(shaped[:, :1])
    return jnp.concatenate([shaped[:, 1:], zero], axis=1).reshape(arr.shape)


def aggregate(proj_all, tiles, target, source, count):
    def single(item):
        proj, tile, dest, anchor = item
        messages = jnp.einsum("tij,tjh->tih", tile.astype(jnp.float32), proj[anchor].astype(jnp.float32), precision=lax.Precision.HIGHEST)
        picker = (dest[None, :] == jnp.arange(count, dtype=jnp.int32)[:, None]).astype(jnp.float32)
        return jnp.einsum("bt,tih->bih", picker, messages, precision=lax.Precision.HIGHEST).astype(jnp.bfloat16)
    return lax.map(single, (proj_all, tiles, target, source))


def advance(blocks, summed, own_weight, near_weight):
    width = blocks.shape[-1]
    flat = blocks.reshape(-1, width)
    mixed = jnp.dot(flat, own_weight, preferred_element_type=jnp.float32) + jnp.dot(summed.reshape(-1, width), near_weight, preferred_element_type=jnp.float32)
    return (flat.astype(jnp.float32) + jax.nn.silu(mixed)).astype(jnp.bfloat16).reshape(blocks.shape)


def project(blocks, matrix):
    width = blocks.shape[-1]
    return jnp.dot(blocks.reshape(-1, width), matrix, preferred_element_type=jnp.float32).astype(jnp.bfloat16).reshape(blocks.shape)


def reference(nodes, fine_tiles, fine_target, fine_source, halo_ids, pool_map, pool_weight, coarse_tiles, coarse_target, coarse_source, weights):
    width = nodes.shape[1]
    blocks = nodes.reshape(DEVICES, NB, BLK, width)
    ftiles = fine_tiles.reshape(DEVICES, ET, BLK, BLK)
    ftarget = fine_target.reshape(DEVICES, ET)
    fsource = fine_source.reshape(DEVICES, ET)
    pick = jax.vmap(lambda block_set, index: block_set[index])
    for turn in range(ROUNDS):
        proj = project(blocks, weights[0])
        leftward = pick(proj, halo_ids[:, 0])
        rightward = pick(proj, halo_ids[:, 1])
        proj_all = jnp.concatenate([proj, from_prev(rightward, 1), from_next(leftward, 1)], axis=1)
        summed = aggregate(proj_all, ftiles, ftarget, fsource, NB)
        blocks = advance(blocks, summed, weights[1], weights[2])
    skipped = blocks
    scaled = blocks.astype(jnp.float32) * pool_weight.reshape(DEVICES, NB, BLK, 1).astype(jnp.float32)
    mapping = pool_map.reshape(DEVICES, NB)
    picker = (mapping[:, None, :] == jnp.arange(3 * NC, dtype=jnp.int32)[None, :, None]).astype(jnp.float32)
    shares = lax.map(lambda item: jnp.einsum("cb,bih->cih", item[0], item[1], precision=lax.Precision.HIGHEST), (picker, scaled))
    coarse = (shares[:, NC:2 * NC] + from_prev(shares[:, 2 * NC:], N_SECT) + from_next(shares[:, :NC], N_SECT)).astype(jnp.bfloat16)
    ctiles = coarse_tiles.reshape(DEVICES, CT, BLK, BLK)
    ctarget = coarse_target.reshape(DEVICES, CT)
    csource = coarse_source.reshape(DEVICES, CT)
    for turn in range(ROUNDS):
        proj = project(coarse, weights[3])
        proj_all = jnp.concatenate([from_prev(proj, N_SECT), proj, from_next(proj, N_SECT)], axis=1)
        summed = aggregate(proj_all, ctiles, ctarget, csource, NC)
        coarse = advance(coarse, summed, weights[4], weights[5])
    beside_all = jnp.concatenate([from_prev(coarse, N_SECT), coarse, from_next(coarse, N_SECT)], axis=1)
    lifted = pick(beside_all, mapping)
    result = skipped.reshape(-1, width).astype(jnp.float32) + jnp.dot(lifted.reshape(-1, width), weights[6], preferred_element_type=jnp.float32)
    return result.astype(jnp.bfloat16)
```

```python
import jax
import jax.numpy as jnp
from jax import lax
from jax.experimental import pallas as pl
from jax.experimental.pallas import tpu as pltpu
from jax.sharding import Mesh, PartitionSpec as P

E = 128
NB = 8
HB = 2
NC = 2
W = 512
HALF = 256
SPLIT = ("zh", "core", "y", "x", "zl")
CHAIN = ("zh", "core", "y", "x", "zl")
DOM = ("y", "x", "zl")
F32 = jnp.float32
BF16 = jnp.bfloat16
VMEM = pl.BlockSpec(memory_space=pltpu.VMEM)
SMEM = pl.BlockSpec(memory_space=pltpu.SMEM)


def shape(rows, dtype=BF16):
    return jax.ShapeDtypeStruct((rows, W), dtype)


def call(body, outs, specs, scratch, flops, data):
    return pl.pallas_call(
        body,
        out_shape=outs,
        in_specs=specs,
        out_specs=[VMEM] * len(outs),
        scratch_shapes=scratch,
        compiler_params=pltpu.CompilerParams(vmem_limit_bytes=40 * 1024 * 1024),
        cost_estimate=pl.CostEstimate(flops=flops, bytes_accessed=data, transcendentals=0),
    )


def rows_at(index, count=E):
    return pl.ds(pl.multiple_of(index * E, E), count)


def dot(a, b):
    return jnp.dot(a, b, preferred_element_type=F32)


def silu(v):
    half = 0.5 * v
    return half + half * jnp.tanh(half)


def add_tiles(tiles, target, source, blocks, total):
    total[...] = jnp.zeros_like(total)
    for t in range(tiles.shape[0]):
        total[rows_at(target[t]), :] += dot(tiles[t], blocks[rows_at(source[t]), :])


def place(core, mine, other, index, full):
    piece = mine[:, index].reshape(W, HALF)
    full[:, pl.ds(pl.multiple_of(core * HALF, HALF), HALF)] = piece
    piece = other[:, index].reshape(W, HALF)
    full[:, pl.ds(pl.multiple_of((1 - core) * HALF, HALF), HALF)] = piece


def first_sums(target, source, halo, nodes, before, after, tiles, summed, left, right, blocks, total):
    blocks[: NB * E, :] = nodes[...]
    blocks[NB * E : (NB + HB) * E, :] = before[...]
    blocks[(NB + HB) * E :, :] = after[...]
    add_tiles(tiles, target, source, blocks, total)
    summed[...] = total[...].astype(BF16)
    for k in range(HB):
        left[k * E : (k + 1) * E, :] = summed[rows_at(halo[k]), :]
        right[k * E : (k + 1) * E, :] = summed[rows_at(halo[HB + k]), :]


def step_rows(blocks, sums, own, near, out, start, count):
    at = slice(start, start + count)
    old = blocks[at, :]
    mixed = dot(old, own[...]) + dot(sums[at, :], near[...])
    out[at, :] = (old.astype(F32) + silu(mixed)).astype(BF16)


def fine_rounds(
    core, target, source, pooled, nodes, before, after, summed, sum_before, sum_after, tiles, mine, other, scale,
    skip, left, middle, right,
    blocks, sums, total, message, own, near, both, shares,
):
    place(core[0], mine, other, 0, message)
    place(core[0], mine, other, 1, own)
    place(core[0], mine, other, 2, near)
    both[...] = dot(message[...], near[...]).astype(BF16)
    blocks[: NB * E, :] = nodes[...]
    blocks[NB * E : (NB + HB) * E, :] = before[...]
    blocks[(NB + HB) * E :, :] = after[...]
    sums[: NB * E, :] = summed[...]
    sums[NB * E : (NB + HB) * E, :] = sum_before[...]
    sums[(NB + HB) * E :, :] = sum_after[...]
    for start in range(0, (NB + 2 * HB) * E, 256):
        step_rows(blocks, sums, own, both, blocks, start, 256)
    add_tiles(tiles, target, source, blocks, total)
    sums[: NB * E, :] = total[...].astype(BF16)
    for start in range(0, NB * E, 256):
        step_rows(blocks, sums, own, both, skip, start, 256)
    factors = scale[...].T
    shares[...] = jnp.zeros_like(shares)
    for f in range(NB):
        block = skip[f * E : (f + 1) * E, :].astype(F32)
        shares[rows_at(pooled[f]), :] += block * factors[:, f : f + 1]
    left[...] = shares[: NC * E, :].astype(BF16)
    middle[...] = shares[NC * E : 2 * NC * E, :]
    right[...] = shares[2 * NC * E :, :].astype(BF16)


def join_coarse(core, mine, other, own, both, lift, message, near):
    place(core[0], mine, other, 0, message)
    place(core[0], mine, other, 1, own)
    place(core[0], mine, other, 2, near)
    place(core[0], mine, other, 3, lift)
    both[...] = dot(message[...], near[...]).astype(BF16)


def coarse_round(target, source, state, before, after, tiles, own, both, out, blocks, total):
    blocks[: NC * E, :] = before[...]
    blocks[NC * E : 2 * NC * E, :] = state[...]
    blocks[2 * NC * E :, :] = after[...]
    add_tiles(tiles, target, source, blocks, total)
    old = state[...]
    mixed = dot(old, own[...]) + dot(total[...].astype(BF16), both[...])
    out[...] = (old.astype(F32) + silu(mixed)).astype(BF16)


def lift_back(pooled, skip, state, before, after, lift, out, lifted):
    lifted[: NC * E, :] = dot(before[...], lift[...])
    lifted[NC * E : 2 * NC * E, :] = dot(state[...], lift[...])
    lifted[2 * NC * E :, :] = dot(after[...], lift[...])
    for f in range(NB):
        at = slice(f * E, (f + 1) * E)
        out[at, :] = (skip[at, :].astype(F32) + lifted[rows_at(pooled[f]), :]).astype(BF16)


def exchange(to_before, to_after, axes):
    count = 1
    for axis in axes:
        count *= lax.axis_size(axis)
    up = [(i, i + 1) for i in range(count - 1)]
    down = [(b, a) for a, b in up]
    return lax.ppermute(to_after, axes, up), lax.ppermute(to_before, axes, down)


def spread(piece, axes):
    count = 1
    for axis in axes:
        count *= lax.axis_size(axis)
    return lax.all_to_all(jnp.broadcast_to(piece[None], (count,) + piece.shape), axes, 0, 0)


def on_device(
    nodes,
    fine_tiles,
    fine_target,
    fine_source,
    halo_ids,
    pool_map,
    pool_weight,
    coarse_tiles,
    coarse_target,
    coarse_source,
    weights,
):
    core = lax.axis_index("core").astype(jnp.int32)
    halo = halo_ids.reshape(-1)
    blocks = nodes.reshape(NB, E, W)
    to_before = blocks[halo[:HB]].reshape(-1, W)
    to_after = blocks[halo[HB:]].reshape(-1, W)
    before, after = exchange(to_before, to_after, CHAIN)

    half = lax.dynamic_slice_in_dim(weights, core * HALF, HALF, axis=2)
    column = spread(half, ("zl",)).transpose(1, 0, 2, 3).reshape(7, -1, HALF)
    fine_mine = spread(column[:3], ("y", "x"))
    fine_other = lax.ppermute(fine_mine, "core", [(0, 1), (1, 0)])

    tile_bytes = 2 * fine_tiles.size
    summed, sums_left, sums_right = call(
        first_sums,
        [shape(NB * E), shape(HB * E), shape(HB * E)],
        [SMEM] * 3 + [VMEM] * 4,
        [pltpu.VMEM(((NB + 2 * HB) * E, W), BF16), pltpu.VMEM((NB * E, W), F32)],
        2 * 24 * E * E * W,
        tile_bytes + 3 * NB * E * W,
    )(fine_target, fine_source, halo, nodes, before, after, fine_tiles)
    sum_before, sum_after = exchange(sums_left, sums_right, CHAIN)

    coarse_mine = spread(column[3:], ("y", "x"))
    coarse_other = lax.ppermute(coarse_mine, "core", [(0, 1), (1, 0)])

    square = pltpu.VMEM((W, W), BF16)
    skip, left, middle, right = call(
        fine_rounds,
        [shape(NB * E), shape(NC * E), shape(NC * E, F32), shape(NC * E)],
        [SMEM] * 4 + [VMEM] * 10,
        [
            pltpu.VMEM(((NB + 2 * HB) * E, W), BF16),
            pltpu.VMEM(((NB + 2 * HB) * E, W), BF16),
            pltpu.VMEM((NB * E, W), F32),
            square,
            square,
            square,
            square,
            pltpu.VMEM((3 * NC * E, W), F32),
        ],
        2 * 24 * E * E * W + 2 * 5 * NB * E * W * W,
        tile_bytes + 8 * NB * E * W,
    )(
        core.reshape(1),
        fine_target,
        fine_source,
        pool_map,
        nodes,
        before,
        after,
        summed,
        sum_before,
        sum_after,
        fine_tiles,
        fine_mine,
        fine_other,
        pool_weight.reshape(NB, E).astype(F32),
    )
    from_before, from_after = exchange(left, right, DOM)
    state = (middle + from_before.astype(F32) + from_after.astype(F32)).astype(BF16)

    own, both, lift = call(
        join_coarse,
        [shape(W), shape(W), shape(W)],
        [SMEM] + [VMEM] * 2,
        [square, square],
        2 * W * W * W,
        8 * 2 * W * W,
    )(core.reshape(1), coarse_mine, coarse_other)
    for turn in range(2):
        near = exchange(state, state, DOM)
        (state,) = call(
            coarse_round,
            [shape(NC * E)],
            [SMEM] * 2 + [VMEM] * 6,
            [pltpu.VMEM((3 * NC * E, W), BF16), pltpu.VMEM((NC * E, W), F32)],
            2 * 6 * E * E * W + 4 * NC * E * W * W,
            2 * coarse_tiles.size + 4 * W * W,
        )(coarse_target, coarse_source, state, *near, coarse_tiles, own, both)
    near = exchange(state, state, DOM)
    (result,) = call(
        lift_back,
        [shape(NB * E)],
        [SMEM] + [VMEM] * 5,
        [pltpu.VMEM((3 * NC * E, W), F32)],
        2 * 3 * NC * E * W * W,
        4 * NB * E * W,
    )(pool_map, skip, state, *near, lift)
    return result


def solution(mesh):
    fine = Mesh(mesh.devices.reshape(4, 2, 4, 4, 4), SPLIT)
    return jax.shard_map(
        on_device,
        mesh=fine,
        in_specs=(
            P(SPLIT, None),
            P(SPLIT, None, None),
            P(SPLIT),
            P(SPLIT),
            P(SPLIT, None, None),
            P(SPLIT),
            P(SPLIT),
            P(SPLIT, None, None),
            P(SPLIT),
            P(SPLIT),
            P(None, DOM, None),
        ),
        out_specs=P(SPLIT, None),
        check_vma=False,
    )
```
